128 devices in a mesh: row: 8 (over x_lo, z), col: 8 (over y, x_hi), depth: 2 (over core).
Axes of the slice: x: 4 (x_hi: 2, x_lo: 2; x = x_hi * 2 + x_lo), y: 4, z: 4, core: 2. Of those that a mesh axis runs over, the one named last changes fastest.
Arguments:
- tokens: bfloat16 [2048, 12288], P('col', ('row', 'depth')), may hold values from -6 to 6
- up_weight: bfloat16 [12288, 24576], P(('row', 'depth'), 'col'), may hold values from -0.0546875 to 0.0546875
- up_bias: float32 [24576], P('col'), may hold values from -3 to 3
- down_weight: bfloat16 [24576, 12288], P('col', ('row', 'depth')), may hold values from -0.0390625 to 0.0390625
- down_bias: float32 [12288], P(('row', 'depth')), may hold values from -3 to 3
Outputs:
- block_output: float32 [2048, 12288], P('col', ('row', 'depth'))
The draws below stay inside these ranges and needn't reach their ends.
All inputs are finite; a program needn't handle non-finite values.
Results may differ from the reference program's by a relative error of at most 0.0025.
Values may be sent and summed in bfloat16 or wider, within the bound.
No kernel may reach another device: no remote copies, remote signals or barrier semaphores. Data moves between devices by JAX's collectives and lax.ppermute only.
A program may use at most 128 MiB of HBM per device.

```python
import jax
import jax.numpy as jnp

D = 12288
FF = 24576
TOKENS = 2048


def raised(result, key, source, target, blocks, factor):
    owner, partner = [(jnp.arange(result.shape[position]) // (result.shape[position] // blocks)).reshape([-1 if axis == position else 1 for axis in range(result.ndim)]) for position in (source, target)]
    chosen = jax.random.permutation(key, blocks)[partner]
    strong = (owner == chosen) | (owner == (partner + blocks // 2) % blocks)
    return jnp.where(strong, factor * result, result)


def levels(stream_key, dims, split, least, largest):
    gain, own = 1.0, jax.random.fold_in(stream_key, 6)
    for position, parts in split:
        heights = jnp.exp(jax.random.uniform(jax.random.fold_in(own, position), (parts,), jnp.float32, least / len(split), largest / len(split)))
        gain = gain * jnp.repeat(heights, dims[position] // parts).reshape([-1 if axis == position else 1 for axis in range(len(dims))])
    return gain


def noise(own_key, extent, spread, bound, pieces=(), dtype=jnp.bfloat16):
    level = levels(own_key, extent, pieces, -0.22, 0.18) if pieces else 1.0
    array = jax.random.normal(own_key, extent, jnp.float32) * spread * level
    return jnp.minimum(jnp.maximum(array, -bound), bound).astype(dtype)


def gaussian_with(stream_key, extent, scale, bound, shards, heavy, held_as=jnp.bfloat16):
    values = scale * jax.random.normal(stream_key, extent, jnp.float32)
    if shards:
        values = values * levels(stream_key, extent, shards, -0.22, 0.18)
    return jnp.clip(raised(values, jax.random.fold_in(stream_key, 3), *heavy), -bound, bound).astype(held_as)


def setup_inputs(seed: int = 0) -> dict:
    key_of = jax.random.split(jax.random.key(seed), 6)
    tokens = gaussian_with(key_of[0], (TOKENS, D), 1.0, 6.0, ((0, 8), (1, 16)), (1, 0, 16, 2.0))
    up_weight = noise(key_of[1], (D, FF), D ** -0.5, 0.0546875, ((0, 16), (1, 8)))
    up_bias = noise(key_of[2], (FF,), 0.5, 3.0, ((0, 8),), jnp.float32)
    down_weight = noise(key_of[3], (FF, D), FF ** -0.5, 0.0390625, ((0, 8), (1, 16)))
    down_bias = noise(key_of[4], (D,), 0.5, 3.0, ((0, 16),), jnp.float32)
    return dict(tokens=tokens, up_weight=up_weight, up_bias=up_bias, down_weight=down_weight, down_bias=down_bias)


def reference(tokens, up_weight, up_bias, down_weight, down_bias):
    pre_act = jnp.dot(tokens, up_weight, preferred_element_type=jnp.float32) + up_bias
    activation = jax.nn.gelu(pre_act, approximate=True).astype(jnp.bfloat16)
    summed = jnp.dot(activation, down_weight, preferred_element_type=jnp.float32) + down_bias
    return summed.astype(jnp.float32)
```

```python
import jax
import jax.numpy as jnp
from jax import lax
from jax.sharding import PartitionSpec as P

BF, F16, F32 = jnp.bfloat16, jnp.float16, jnp.float32
SCALE = 16.0

ROW = {
    "x": [(i, i ^ 4) for i in range(8)],
    "a": [(i, i ^ 1) for i in range(8)],
    "b": [(i, i ^ 3) for i in range(8)],
}
COL = {
    "x": [(i, i ^ 1) for i in range(8)],
    "a": [(i, i ^ 2) for i in range(8)],
    "b": [(i, i ^ 6) for i in range(8)],
}
SWAP = [(0, 1), (1, 0)]

CHUNKS = (
    (2, "abx", "xab", "abx"),
    (2, "bxa", "xba", "bax"),
    (2, "xab", "xab", "abx"),
    (2, "abx", "xba", "bax"),
)


def gather_tokens(piece, order, layout, flip):
    u, k = piece.shape
    held, dims = piece, ""
    for d in order:
        other = lax.ppermute(held, "col", COL[d])
        new = "".join(c for c in layout if c in dims + d)
        at = new.index(d)
        shape = (2 ** at, held.shape[0] // 2 ** at, k)
        mine, theirs = held.reshape(shape), other.reshape(shape)
        low = jnp.where(flip[d], theirs, mine)
        high = jnp.where(flip[d], mine, theirs)
        held = jnp.stack([low, high], 1).reshape(-1, k)
        dims = new
    return held


def sum_rows(partial, layout):
    held = partial
    for d in layout:
        half = held.shape[0] // 2
        got = lax.ppermute(held[half:].astype(F16), "row", ROW[d])
        held = held[:half].astype(F32) + got.astype(F32)
    return held


def gather_rows(block, layout):
    held = block
    for d in reversed(layout):
        held = jnp.concatenate([held, lax.ppermute(held, "row", ROW[d])], 0)
    return held


def sum_cols(terms, order, layout, flip):
    held, dims = terms, layout
    for d in order:
        at = dims.index(d)
        s = held.shape
        v = held.reshape(2, 2 ** at, 2, s[1] // 2 ** (at + 1), s[2])
        low, high = v[:, :, 0], v[:, :, 1]
        send = jnp.where(flip[d], low, high).astype(BF)
        keep = jnp.where(flip[d], high, low)
        got = lax.ppermute(send.reshape(2, s[1] // 2, s[2]), "col", COL[d])
        held = keep.reshape(2, s[1] // 2, s[2]) + got.astype(F32)
        dims = dims.replace(d, "")
    return held


def body(tokens, up_weight, up_bias, down_weight, down_bias):
    row, col, depth = (lax.axis_index(a) for a in ("row", "col", "depth"))
    zy = (row % 4) ^ (col // 2)
    b_bit = zy // 2
    flip = {"x": ((row // 4) ^ (col % 2)) == 1, "a": ((zy % 2) ^ b_bit) == 1, "b": b_bit == 1}
    half = tokens.shape[0] // 2

    give = lax.dynamic_slice_in_dim(tokens, (1 - depth) * half, half, 0)
    keep = lax.dynamic_slice_in_dim(tokens, depth * half, half, 0)
    mine = jnp.concatenate([keep, lax.ppermute(give, "depth", SWAP)], 1)
    up = jnp.concatenate([up_weight, lax.ppermute(up_weight, "depth", SWAP)], 0)
    down_other = lax.ppermute(down_weight, "depth", SWAP)

    own, other, at = [], [], 0
    for units, layout, token_order, out_order in CHUNKS:
        u = 16 * units
        x = gather_tokens(mine[at : at + u], token_order, layout, flip)
        at += u
        partial = (SCALE * jnp.dot(x, up, preferred_element_type=F32)).astype(F16)
        summed = sum_rows(partial, layout) * (1 / SCALE)
        act = jax.nn.gelu(summed + up_bias, approximate=True).astype(BF)
        act = gather_rows(act, layout)
        terms = jnp.stack([jnp.dot(act, w, preferred_element_type=F32) for w in (down_weight, down_other)])
        out = sum_cols(terms, out_order, layout, flip)
        own.append(out[0])
        other.append(out[1])
    own, other = jnp.concatenate(own, 0), jnp.concatenate(other, 0)
    got = lax.ppermute(other, "depth", SWAP)
    first = jnp.where(depth == 0, own, got)
    last = jnp.where(depth == 0, got, own)
    return jnp.concatenate([first, last], 0) + down_bias


def solution(mesh):
    placed = (
        P("col", ("row", "depth")),
        P(("row", "depth"), "col"),
        P("col"),
        P("col", ("row", "depth")),
        P(("row", "depth")),
    )
    return jax.shard_map(
        body, mesh=mesh, in_specs=placed, out_specs=P("col", ("row", "depth")), check_vma=False
    )
```

```python
import jax
import jax.numpy as jnp
from jax import lax
from jax.sharding import PartitionSpec as P

BF, F16, F32 = jnp.bfloat16, jnp.float16, jnp.float32
SCALE = 16.0

ROW = {
    "x": [(i, i ^ 8) for i in range(16)],
    "p": [(i, i ^ (6 if i & 1 else 2)) for i in range(16)],
    "q": [(i, i ^ (2 if i & 1 else 6)) for i in range(16)],
}
COL = {
    "x": [(i, i ^ 2) for i in range(16)],
    "p": [(i, i ^ (12 if i & 1 else 4)) for i in range(16)],
    "q": [(i, i ^ (4 if i & 1 else 12)) for i in range(16)],
}
SWAP = [(0, 1), (1, 0)]

UNITS = (3, 3, 2)
LAYOUTS = ('pxq', 'pxq', 'pxq')
TOKEN_ORDER, OUT_ORDER = "xpq", "pqx"
ORDER = tuple(map(int, "013201012302102102010121202130102120212102"))


def row_swap(v, d):
    return lax.ppermute(v, ("row", "depth"), ROW[d])


def col_swap(v, d):
    return lax.ppermute(v, ("col", "depth"), COL[d])


class Chain:
    def __init__(self, token):
        self.token = token

    def after(self, *values):
        *values, self.token = lax.optimization_barrier((*values, self.token))
        return values[0] if len(values) == 1 else values


def chunk(chain, piece, up, up_bias, down, flip, layout, results):
    u, k = piece.shape
    held, dims = chain.after(piece), ""
    for d in TOKEN_ORDER:
        other = col_swap(chain.after(held), d)
        yield
        held, other = chain.after(held, other)
        new = "".join(c for c in layout if c in dims + d)
        at = new.index(d)
        shape = (2**at, held.shape[0] // 2**at, k)
        mine, theirs = held.reshape(shape), other.reshape(shape)
        low = jnp.where(flip[d], theirs, mine)
        high = jnp.where(flip[d], mine, theirs)
        held = chain.after(jnp.stack([low, high], 1).reshape(-1, k))
        dims = new
    half = k // 2
    partial = jnp.dot(held[:, :half], up[0], preferred_element_type=F32)
    partial = SCALE * (partial + jnp.dot(held[:, half:], up[1], preferred_element_type=F32))
    rows = partial.shape[0] // 2
    held, send = partial[:rows], partial[rows:].astype(F16)
    for d in layout:
        if d != layout[0]:
            rows = held.shape[0] // 2
            send, held = held[rows:], held[:rows]
        send, held = chain.after(send.astype(F16), held)
        got = row_swap(send, d)
        yield
        held, got = chain.after(held, got)
        held = held + got.astype(F32)
    held = jax.nn.gelu(held * (1 / SCALE) + up_bias, approximate=True).astype(BF)
    for d in reversed(layout):
        other = row_swap(chain.after(held), d)
        yield
        held, other = chain.after(held, other)
        held = chain.after(jnp.concatenate([held, other], 0))
    held, dims = jnp.stack([jnp.dot(held, w, preferred_element_type=F32) for w in down]), layout
    for d in OUT_ORDER:
        at, (_, rows, n) = dims.index(d), held.shape
        parts = held.reshape(2, 2**at, 2, rows // 2 ** (at + 1), n)
        low, high = parts[:, :, 0], parts[:, :, 1]
        send = jnp.where(flip[d], low, high).astype(BF).reshape(2, rows // 2, n)
        held = jnp.where(flip[d], high, low).reshape(2, rows // 2, n)
        send, held = chain.after(send, held)
        got = col_swap(send, d)
        yield
        held, got = chain.after(held, got)
        held = held + got.astype(F32)
        dims = dims.replace(d, "")
    results.append(chain.after(held))


def fetch(chain, up, down):
    for w in (up, down):
        other = lax.ppermute(chain.after(w[0]), "depth", SWAP)
        yield
        w.append(chain.after(jnp.where(chain.token, chain.after(other), jnp.zeros_like(other))))


def body(tokens, up_weight, up_bias, down_weight, down_bias):
    row, col, depth = (lax.axis_index(a) for a in ("row", "col", "depth"))
    zy = (row % 4) ^ (col // 2)
    b_bit = zy // 2
    a_bit = (zy % 2) ^ b_bit
    flip = {
        "x": ((row // 4) ^ (col % 2)) == 1,
        "p": jnp.where(depth == 0, a_bit, b_bit) == 1,
        "q": jnp.where(depth == 0, b_bit, a_bit) == 1,
    }
    half = tokens.shape[0] // 2

    give = lax.dynamic_slice_in_dim(tokens, (1 - depth) * half, half, 0)
    keep = lax.dynamic_slice_in_dim(tokens, depth * half, half, 0)
    mine = jnp.concatenate([keep, lax.ppermute(give, "depth", SWAP)], 1)
    chain = Chain(row < 8)
    up, down = [up_weight], [down_weight]
    weights = fetch(chain, up, down)

    results, steps, at = [[] for _ in UNITS], [], 0
    for units, layout, result in zip(UNITS, LAYOUTS, results):
        piece = mine[at : at + 16 * units]
        steps.append(chunk(chain, piece, up, up_bias, down, flip, layout, result))
        at += 16 * units
    steps.append(weights)
    for i in ORDER:
        next(steps[i], None)
    out = jnp.concatenate([r[0] for r in results], 1)
    own, other = out[0], out[1]
    got = lax.ppermute(other, "depth", SWAP)
    first = jnp.where(depth == 0, own, got)
    last = jnp.where(depth == 0, got, own)
    return jnp.where(chain.token, jnp.concatenate([first, last], 0) + down_bias, 0.0)


def solution(mesh):
    placed = (
        P("col", ("row", "depth")),
        P(("row", "depth"), "col"),
        P("col"),
        P("col", ("row", "depth")),
        P(("row", "depth")),
    )
    return jax.shard_map(
        body, mesh=mesh, in_specs=placed, out_specs=P("col", ("row", "depth")), check_vma=False
    )
```

```python
import jax
import jax.numpy as jnp
from jax import lax
from jax.sharding import PartitionSpec as P

BF, F16, F32 = jnp.bfloat16, jnp.float16, jnp.float32
SCALE = 16.0

ROW = {
    "x": [(i, i ^ 8) for i in range(16)],
    "p": [(i, i ^ (6 if i & 1 else 2)) for i in range(16)],
    "q": [(i, i ^ (2 if i & 1 else 6)) for i in range(16)],
}
COL = {
    "x": [(i, i ^ 2) for i in range(16)],
    "p": [(i, i ^ (12 if i & 1 else 4)) for i in range(16)],
    "q": [(i, i ^ (4 if i & 1 else 12)) for i in range(16)],
}
SWAP = [(0, 1), (1, 0)]

UNITS = (2, 2, 2, 2)
LAYOUTS = ("pxq", "pxq", "pxq", "pxq")
TOKEN_ORDER, OUT_ORDER = "xpq", "pqx"
ORDER = tuple(map(int, "0142031202140313021320312013201203243103201310231231230"))


def row_swap(v, d):
    return lax.ppermute(v, ("row", "depth"), ROW[d])


def col_swap(v, d):
    return lax.ppermute(v, ("col", "depth"), COL[d])


class Chain:
    def __init__(self, token):
        self.token = token

    def after(self, *values):
        *values, self.token = lax.optimization_barrier((*values, self.token))
        return values[0] if len(values) == 1 else values


def chunk(chain, piece, up, up_bias, down, flip, layout, results):
    u, k = piece.shape
    held, dims = chain.after(piece), ""
    for d in TOKEN_ORDER:
        other = col_swap(chain.after(held), d)
        yield
        held, other = chain.after(held, other)
        new = "".join(c for c in layout if c in dims + d)
        at = new.index(d)
        shape = (2**at, held.shape[0] // 2**at, k)
        mine, theirs = held.reshape(shape), other.reshape(shape)
        low = jnp.where(flip[d], theirs, mine)
        high = jnp.where(flip[d], mine, theirs)
        held = chain.after(jnp.stack([low, high], 1).reshape(-1, k))
        dims = new
    half = k // 2
    partial = jnp.dot(held[:, :half], up[0], preferred_element_type=F32)
    partial = SCALE * (partial + jnp.dot(held[:, half:], up[1], preferred_element_type=F32))
    rows = partial.shape[0] // 2
    held, send = partial[:rows], partial[rows:].astype(F16)
    for d in layout:
        if d != layout[0]:
            rows = held.shape[0] // 2
            send, held = held[rows:], held[:rows]
        send, held = chain.after(send.astype(F16), held)
        got = row_swap(send, d)
        yield
        held, got = chain.after(held, got)
        held = held + got.astype(F32)
    held = jax.nn.gelu(held * (1 / SCALE) + up_bias, approximate=True).astype(BF)
    for d in reversed(layout):
        other = row_swap(chain.after(held), d)
        yield
        held, other = chain.after(held, other)
        held = chain.after(jnp.concatenate([held, other], 0))
    held, dims = jnp.stack([jnp.dot(held, w, preferred_element_type=F32) for w in down]), layout
    for d in OUT_ORDER:
        at, (_, rows, n) = dims.index(d), held.shape
        parts = held.reshape(2, 2**at, 2, rows // 2 ** (at + 1), n)
        low, high = parts[:, :, 0], parts[:, :, 1]
        send = jnp.where(flip[d], low, high).astype(BF).reshape(2, rows // 2, n)
        held = jnp.where(flip[d], high, low).reshape(2, rows // 2, n)
        send, held = chain.after(send, held)
        got = col_swap(send, d)
        yield
        held, got = chain.after(held, got)
        held = held + got.astype(F32)
        dims = dims.replace(d, "")
    results.append(chain.after(held))


def fetch(chain, up, down):
    for w in (up, down):
        other = lax.ppermute(chain.after(w[0]), "depth", SWAP)
        yield
        w.append(chain.after(jnp.where(chain.token, chain.after(other), jnp.zeros_like(other))))


def body(tokens, up_weight, up_bias, down_weight, down_bias):
    row, col, depth = (lax.axis_index(a) for a in ("row", "col", "depth"))
    zy = (row % 4) ^ (col // 2)
    b_bit = zy // 2
    a_bit = (zy % 2) ^ b_bit
    flip = {
        "x": ((row // 4) ^ (col % 2)) == 1,
        "p": jnp.where(depth == 0, a_bit, b_bit) == 1,
        "q": jnp.where(depth == 0, b_bit, a_bit) == 1,
    }
    half = tokens.shape[0] // 2

    give = lax.dynamic_slice_in_dim(tokens, (1 - depth) * half, half, 0)
    keep = lax.dynamic_slice_in_dim(tokens, depth * half, half, 0)
    mine = jnp.concatenate([keep, lax.ppermute(give, "depth", SWAP)], 1)
    chain = Chain(row < 8)
    up, down = [up_weight], [down_weight]
    weights = fetch(chain, up, down)

    results, steps, at = [[] for _ in UNITS], [], 0
    for units, layout, result in zip(UNITS, LAYOUTS, results):
        piece = mine[at : at + 16 * units]
        steps.append(chunk(chain, piece, up, up_bias, down, flip, layout, result))
        at += 16 * units
    steps.append(weights)
    for i in ORDER:
        next(steps[i], None)
    out = jnp.concatenate([r[0] for r in results], 1)
    own, other = out[0], out[1]
    got = lax.ppermute(other, "depth", SWAP)
    first = jnp.where(depth == 0, own, got)
    last = jnp.where(depth == 0, got, own)
    return jnp.where(chain.token, jnp.concatenate([first, last], 0) + down_bias, 0.0)


def solution(mesh):
    placed = (
        P("col", ("row", "depth")),
        P(("row", "depth"), "col"),
        P("col"),
        P("col", ("row", "depth")),
        P(("row", "depth")),
    )
    return jax.shard_map(
        body, mesh=mesh, in_specs=placed, out_specs=P("col", ("row", "depth")), check_vma=False
    )
```

```python
import jax
import jax.numpy as jnp
from jax import lax
from jax.experimental import pallas as pl
from jax.experimental.pallas import tpu as pltpu
from jax.sharding import PartitionSpec as P

BF, F16, F32 = jnp.bfloat16, jnp.float16, jnp.float32
SCALE = 16.0

ROW = {
    "x": [(i, i ^ 8) for i in range(16)],
    "p": [(i, i ^ (6 if i & 1 else 2)) for i in range(16)],
    "q": [(i, i ^ (2 if i & 1 else 6)) for i in range(16)],
}
COL = {
    "x": [(i, i ^ 2) for i in range(16)],
    "p": [(i, i ^ (12 if i & 1 else 4)) for i in range(16)],
    "q": [(i, i ^ (4 if i & 1 else 12)) for i in range(16)],
}
SWAP = [(0, 1), (1, 0)]

UNITS = (2, 2, 2, 2)
LAYOUTS = ("pxq", "pxq", "pxq", "pxq")
TOKEN_ORDER, OUT_ORDER = "xpq", "pqx"
ORDER = tuple(map(int, "0142031202140313021320312013201203243103201310231231230"))


def row_swap(v, d):
    return lax.ppermute(v, ("row", "depth"), ROW[d])


def col_swap(v, d):
    return lax.ppermute(v, ("col", "depth"), COL[d])


def up_kernel(x, own, other, keep, send):
    k, rows = own.shape[0], keep.shape[0]
    acc = jnp.dot(x[:, :k], own[...], preferred_element_type=F32)
    acc = acc + jnp.dot(x[:, k:], other[...], preferred_element_type=F32)
    acc = SCALE * acc
    keep[...] = acc[:rows]
    send[...] = acc[rows:]


def up_project(x, own, other):
    (m, k2), n, block = x.shape, own.shape[1], 1024
    half = jax.ShapeDtypeStruct((m // 2, n), F32)
    weight = pl.BlockSpec((k2 // 2, block), lambda i: (0, i))
    out = pl.BlockSpec((m // 2, block), lambda i: (0, i))
    return pl.pallas_call(
        up_kernel,
        grid=(n // block,),
        in_specs=[pl.BlockSpec((m, k2), lambda i: (0, 0)), weight, weight],
        out_specs=[out, out],
        out_shape=[half, half],
        compiler_params=pltpu.CompilerParams(vmem_limit_bytes=32 << 20),
    )(x, own, other)


class Chain:
    def __init__(self, token):
        self.token = token

    def after(self, *values):
        *values, self.token = lax.optimization_barrier((*values, self.token))
        return values[0] if len(values) == 1 else values


def chunk(chain, piece, up, up_bias, down, flip, layout, results):
    u, k = piece.shape
    held, dims = chain.after(piece), ""
    for d in TOKEN_ORDER:
        other = col_swap(chain.after(held), d)
        yield
        held, other = chain.after(held, other)
        new = "".join(c for c in layout if c in dims + d)
        at = new.index(d)
        shape = (2**at, held.shape[0] // 2**at, k)
        mine, theirs = held.reshape(shape), other.reshape(shape)
        low = jnp.where(flip[d], theirs, mine)
        high = jnp.where(flip[d], mine, theirs)
        held = chain.after(jnp.stack([low, high], 1).reshape(-1, k))
        dims = new
    held, send = up_project(held, *up)
    for d in layout:
        if d != layout[0]:
            rows = held.shape[0] // 2
            send, held = held[rows:], held[:rows]
        send, held = chain.after(send.astype(F16), held)
        got = row_swap(send, d)
        yield
        held, got = chain.after(held, got)
        held = held + got.astype(F32)
    held = jax.nn.gelu(held * (1 / SCALE) + up_bias, approximate=True).astype(BF)
    for d in reversed(layout):
        other = row_swap(chain.after(held), d)
        yield
        held, other = chain.after(held, other)
        held = chain.after(jnp.concatenate([held, other], 0))
    held, dims = jnp.stack([jnp.dot(held, w, preferred_element_type=F32) for w in down]), layout
    for d in OUT_ORDER:
        at, (_, rows, n) = dims.index(d), held.shape
        parts = held.reshape(2, 2**at, 2, rows // 2 ** (at + 1), n)
        low, high = parts[:, :, 0], parts[:, :, 1]
        send = jnp.where(flip[d], low, high).astype(BF).reshape(2, rows // 2, n)
        held = jnp.where(flip[d], high, low).reshape(2, rows // 2, n)
        send, held = chain.after(send, held)
        got = col_swap(send, d)
        yield
        held, got = chain.after(held, got)
        held = held + got.astype(F32)
        dims = dims.replace(d, "")
    results.append(chain.after(held))


def fetch(chain, up, down):
    for w in (up, down):
        other = lax.ppermute(chain.after(w[0]), "depth", SWAP)
        yield
        w.append(chain.after(jnp.where(chain.token, chain.after(other), jnp.zeros_like(other))))


def body(tokens, up_weight, up_bias, down_weight, down_bias):
    row, col, depth = (lax.axis_index(a) for a in ("row", "col", "depth"))
    zy = (row % 4) ^ (col // 2)
    b_bit = zy // 2
    a_bit = (zy % 2) ^ b_bit
    flip = {
        "x": ((row // 4) ^ (col % 2)) == 1,
        "p": jnp.where(depth == 0, a_bit, b_bit) == 1,
        "q": jnp.where(depth == 0, b_bit, a_bit) == 1,
    }
    half = tokens.shape[0] // 2

    give = lax.dynamic_slice_in_dim(tokens, (1 - depth) * half, half, 0)
    keep = lax.dynamic_slice_in_dim(tokens, depth * half, half, 0)
    mine = jnp.concatenate([keep, lax.ppermute(give, "depth", SWAP)], 1)
    chain = Chain(row < 8)
    up, down = [up_weight], [down_weight]
    weights = fetch(chain, up, down)

    results, steps, at = [[] for _ in UNITS], [], 0
    for units, layout, result in zip(UNITS, LAYOUTS, results):
        piece = mine[at : at + 16 * units]
        steps.append(chunk(chain, piece, up, up_bias, down, flip, layout, result))
        at += 16 * units
    steps.append(weights)
    for i in ORDER:
        next(steps[i], None)
    out = jnp.concatenate([r[0] for r in results], 1)
    own, other = out[0], out[1]
    got = lax.ppermute(other, "depth", SWAP)
    first = jnp.where(depth == 0, own, got)
    last = jnp.where(depth == 0, got, own)
    return jnp.where(chain.token, jnp.concatenate([first, last], 0) + down_bias, 0.0)


def solution(mesh):
    placed = (
        P("col", ("row", "depth")),
        P(("row", "depth"), "col"),
        P("col"),
        P("col", ("row", "depth")),
        P(("row", "depth")),
    )
    return jax.shard_map(
        body, mesh=mesh, in_specs=placed, out_specs=P("col", ("row", "depth")), check_vma=False
    )
```

```python
import jax
import jax.numpy as jnp
from jax import lax
from jax.experimental import pallas as pl
from jax.experimental.pallas import tpu as pltpu
from jax.sharding import PartitionSpec as P

BF, F16, F32 = jnp.bfloat16, jnp.float16, jnp.float32
SCALE = 16.0

ROW = {
    "x": [(i, i ^ 8) for i in range(16)],
    "p": [(i, i ^ (6 if i & 1 else 2)) for i in range(16)],
    "q": [(i, i ^ (2 if i & 1 else 6)) for i in range(16)],
}
COL = {
    "x": [(i, i ^ 2) for i in range(16)],
    "p": [(i, i ^ (12 if i & 1 else 4)) for i in range(16)],
    "q": [(i, i ^ (4 if i & 1 else 12)) for i in range(16)],
}
SWAP = [(0, 1), (1, 0)]

UNITS = (2, 2, 2, 2)
LAYOUTS = ("pxq", "pxq", "pxq", "pxq")
TOKEN_ORDER, OUT_ORDER = "xpq", "pqx"
ORDER = tuple(map(int, "0142031202140313021320312013201203243103201310231231230"))


def row_swap(v, d):
    return lax.ppermute(v, ("row", "depth"), ROW[d])


def col_swap(v, d):
    return lax.ppermute(v, ("col", "depth"), COL[d])


def up_kernel(x, own, other, keep, send):
    k, rows = own.shape[0], keep.shape[0]
    acc = jnp.dot(x[:, :k], own[...], preferred_element_type=F32)
    acc = acc + jnp.dot(x[:, k:], other[...], preferred_element_type=F32)
    acc = SCALE * acc
    keep[...] = acc[:rows]
    send[...] = acc[rows:]


def up_project(x, own, other):
    (m, k2), n, block = x.shape, own.shape[1], 1024
    half = jax.ShapeDtypeStruct((m // 2, n), F32)
    weight = pl.BlockSpec((k2 // 2, block), lambda i: (0, i))
    out = pl.BlockSpec((m // 2, block), lambda i: (0, i))
    return pl.pallas_call(
        up_kernel,
        grid=(n // block,),
        in_specs=[pl.BlockSpec((m, k2), lambda i: (0, 0)), weight, weight],
        out_specs=[out, out],
        out_shape=[half, half],
        compiler_params=pltpu.CompilerParams(vmem_limit_bytes=32 << 20),
    )(x, own, other)


class Chain:
    def __init__(self, token):
        self.token = token

    def after(self, *values):
        *values, self.token = lax.optimization_barrier((*values, self.token))
        return values[0] if len(values) == 1 else values


def chunk(chain, piece, up, up_bias, down, flip, layout, results):
    u, k = piece.shape
    held, dims = chain.after(piece), ""
    for d in TOKEN_ORDER:
        other = col_swap(chain.after(held), d)
        yield
        held, other = chain.after(held, other)
        new = "".join(c for c in layout if c in dims + d)
        at = new.index(d)
        shape = (2**at, held.shape[0] // 2**at, k)
        mine, theirs = held.reshape(shape), other.reshape(shape)
        low = jnp.where(flip[d], theirs, mine)
        high = jnp.where(flip[d], mine, theirs)
        held = chain.after(jnp.stack([low, high], 1).reshape(-1, k))
        dims = new
    held, send = up_project(held, *up)
    for d in layout:
        if d != layout[0]:
            rows = held.shape[0] // 2
            send, held = held[rows:], held[:rows]
        send, held = chain.after(send.astype(F16), held)
        got = row_swap(send, d)
        yield
        held, got = chain.after(held, got)
        held = held + got.astype(F32)
    held = jax.nn.gelu(held * (1 / SCALE) + up_bias, approximate=True).astype(BF)
    for d in reversed(layout):
        other = row_swap(chain.after(held), d)
        yield
        held, other = chain.after(held, other)
        held = chain.after(jnp.concatenate([held, other], 0))
    held, dims = jnp.stack([jnp.dot(held, w, preferred_element_type=F32) for w in down]), layout
    for d in OUT_ORDER:
        at, (_, rows, n) = dims.index(d), held.shape
        parts = held.reshape(2, 2**at, 2, rows // 2 ** (at + 1), n)
        low, high = parts[:, :, 0], parts[:, :, 1]
        send = jnp.where(flip[d], low, high).astype(BF).reshape(2, rows // 2, n)
        held = jnp.where(flip[d], high, low).reshape(2, rows // 2, n)
        send, held = chain.after(send, held)
        got = col_swap(send, d)
        yield
        held, got = chain.after(held, got)
        held = held + got.astype(F32)
        dims = dims.replace(d, "")
    results.append(chain.after(held))


def fetch(chain, up, down):
    for w in (up, down):
        other = lax.ppermute(chain.after(w[0]), "depth", SWAP)
        yield
        other = chain.after(other)
        if w is down:
            other = chain.after(jnp.where(chain.token, other, jnp.zeros_like(other)))
        w.append(other)


def body(tokens, up_weight, up_bias, down_weight, down_bias):
    row, col, depth = (lax.axis_index(a) for a in ("row", "col", "depth"))
    zy = (row % 4) ^ (col // 2)
    b_bit = zy // 2
    a_bit = (zy % 2) ^ b_bit
    flip = {
        "x": ((row // 4) ^ (col % 2)) == 1,
        "p": jnp.where(depth == 0, a_bit, b_bit) == 1,
        "q": jnp.where(depth == 0, b_bit, a_bit) == 1,
    }
    half = tokens.shape[0] // 2

    give = lax.dynamic_slice_in_dim(tokens, (1 - depth) * half, half, 0)
    keep = lax.dynamic_slice_in_dim(tokens, depth * half, half, 0)
    mine = jnp.concatenate([keep, lax.ppermute(give, "depth", SWAP)], 1)
    chain = Chain(row < 8)
    up, down = [up_weight], [down_weight]
    weights = fetch(chain, up, down)

    results, steps, at = [[] for _ in UNITS], [], 0
    for units, layout, result in zip(UNITS, LAYOUTS, results):
        piece = mine[at : at + 16 * units]
        steps.append(chunk(chain, piece, up, up_bias, down, flip, layout, result))
        at += 16 * units
    steps.append(weights)
    for i in ORDER:
        next(steps[i], None)
    out = jnp.concatenate([r[0] for r in results], 1)
    own, other = out[0], out[1]
    got = lax.ppermute(other, "depth", SWAP)
    first = jnp.where(depth == 0, own, got)
    last = jnp.where(depth == 0, got, own)
    return jnp.where(chain.token, jnp.concatenate([first, last], 0) + down_bias, 0.0)


def solution(mesh):
    placed = (
        P("col", ("row", "depth")),
        P(("row", "depth"), "col"),
        P("col"),
        P("col", ("row", "depth")),
        P(("row", "depth")),
    )
    return jax.shard_map(
        body, mesh=mesh, in_specs=placed, out_specs=P("col", ("row", "depth")), check_vma=False
    )
```
